32 devices in a mesh: half: 2 (over core), cls: 2 (over y), img: 8 (over z, x).
Axes of the slice: x: 2, y: 2, z: 4, core: 2. Of those that a mesh axis runs over, the one named last changes fastest.
Arguments:
- images: bfloat16 [2, 4096, 2, 8320], P('half', ('cls', 'img')), may hold values from -8 to 8
- projections: bfloat16 [2, 8, 8, 2, 8320], P('half', 'cls', None, None, 'img'), may hold values from -8 to 8
- ctf_table: float32 [2, 32, 8320], P('half'), may hold values from -1 to 1
- ctf_group: int32 [2, 4096], P('half', ('cls', 'img')), may hold values from 0 to 31
- orient_ids: int32 [2, 4096, 4], P('half', ('cls', 'img')), may hold values from 0 to 7
- trans_ids: int32 [2, 8], P('half'), may hold values from 0 to 24
- inv_sigma: float32 [2, 8320], P('half'), may hold values from 0.5 to 2
- counts: int32 [2, 16], P('half', ('cls', 'img')), may hold values from 1 to 256, 2560 in all within a row
Outputs:
- posterior: bfloat16 [2, 4096, 512], P('half', ('cls', 'img'))
- slab: float32 [2, 8, 8, 2, 8320], P('half', 'cls', None, None, 'img')
- fsc_map: float32 [2, 8, 8, 8320], P('half', 'cls', None, 'img')
The draws below stay inside these ranges and needn't reach their ends.
Inputs may be any that keep to these rules, and one draw needn't show every extreme that they name: counts[h, s] is the number of live particles of shard s, held in its first slots; each half-set's counts sum to 2560, and the largest is 256.
All inputs are finite; a program needn't handle non-finite values.
Results may differ from the reference program's by a relative error of at most 0.013.
The reference program's roundings to bfloat16 on the way count: a program that leaves them out, or rounds other values in their place, can miss the bound.
Values may be sent and summed in bfloat16 or wider, within the bound.
A program may use at most 192 MiB of HBM per device.

```python
import math
import jax
import jax.numpy as jnp
import numpy as np
from jax import lax

K = 8
BOX = 128
FC = 8320
O = 8
TR = 8
TGRID = 5
NLOCAL = 4
G = 32
PART_DEV = 256
SHARDS = 16
PARTICLES = 4096
LIVE = 2560


ctf_square_mean = 1.0 / 3.0


inverse_mean = 1.5 / math.log(4.0)


def shared_integers(key):
    groups = jax.random.randint(jax.random.fold_in(key, 11), (2, PARTICLES), 0, G, dtype=jnp.int32)
    orients = jax.random.randint(jax.random.fold_in(key, 12), (2, PARTICLES, NLOCAL), 0, O, dtype=jnp.int32)
    shifts = jax.random.randint(jax.random.fold_in(key, 13), (2, TR), 0, TGRID * TGRID, dtype=jnp.int32)
    target_class = jax.random.randint(jax.random.fold_in(key, 14), (2, PARTICLES), 0, K, dtype=jnp.int32)
    target_slot = jax.random.randint(jax.random.fold_in(key, 15), (2, PARTICLES), 0, TR, dtype=jnp.int32)
    return (groups, orients, shifts, target_class, target_slot)


def make_ctf(key):
    return jax.random.uniform(jax.random.fold_in(key, 21), (2, G, FC), jnp.float32, -1.0, 1.0)


def make_projections(key):
    normal_part = jnp.clip(jax.random.normal(jax.random.fold_in(key, 31), (2, K, O, 2, FC), jnp.float32), -4.0, 4.0)
    target_norm = jnp.exp(jax.random.uniform(jax.random.fold_in(key, 32), (2, K, O), jnp.float32, math.log(4.0), math.log(12.0)))
    scales = jnp.sqrt(target_norm / (2.0 * FC * ctf_square_mean * inverse_mean))
    sections = normal_part * scales[:, :, :, None, None]
    return sections


def draw_images(key, part):
    groups, orients, shifts, target_class, target_slot = shared_integers(key)
    ctf_values = make_ctf(key)
    sections = make_projections(key)
    target_orient = orients[:, :, 0]
    flat_sections = sections.reshape(2, K * O, 2, FC)
    chosen = jnp.take_along_axis(flat_sections, (target_class * O + target_orient)[:, :, None, None], axis=1)
    ctf_rows = jnp.take_along_axis(ctf_values, groups[:, :, None], axis=1)
    shift_value = jnp.take_along_axis(shifts, target_slot, axis=1)
    half_width = BOX // 2 + 1
    freq_index = jnp.arange(FC, dtype=jnp.int32)
    row_index = freq_index // half_width
    wave_x = (row_index - BOX * (row_index >= BOX // 2).astype(jnp.int32)).astype(jnp.float32)
    wave_y = (freq_index % half_width).astype(jnp.float32)
    shift_x = (shift_value % TGRID - TGRID // 2).astype(jnp.float32)
    shift_y = (shift_value // TGRID - TGRID // 2).astype(jnp.float32)
    angle = 2.0 * math.pi / BOX * (shift_x[:, :, None] * wave_x[None, None, :] + shift_y[:, :, None] * wave_y[None, None, :])
    cosine = jnp.cos(angle)
    sine = jnp.sin(angle)
    real_part = chosen[:, :, 0, :]
    imag_part = chosen[:, :, 1, :]
    signal = ctf_rows[:, :, None, :] * jnp.stack([real_part * cosine - imag_part * sine, real_part * sine + imag_part * cosine], axis=2)
    noise = jnp.clip(jax.random.normal(jax.random.fold_in(key, 41), (2, PARTICLES, 2, FC), jnp.float32), -5.0, 5.0)
    return (noise + 0.5 * signal).astype(jnp.bfloat16)


def draw_projections(key, part):
    return make_projections(key).astype(jnp.bfloat16)


def draw_ctf_table(key, part):
    return make_ctf(key)


def draw_ctf_group(key, part):
    return shared_integers(key)[0]


def draw_orient_ids(key, part):
    return shared_integers(key)[1]


def draw_trans_ids(key, part):
    return shared_integers(key)[2]


def block_scale(key, dims, split, least, high):
    gain = 1.0
    for dim, parts in split:
        heights = jax.random.uniform(jax.random.fold_in(jax.random.fold_in(key, 6), dim), (parts,), jnp.float32, least / len(split), high / len(split))
        gain = gain * jnp.repeat(jnp.exp(heights), dims[dim] // parts).reshape((-1,) + (1,) * (len(dims) - 1 - dim))
    return gain


def split_up(amount, total, most, skew):
    loads = [(1 << 20) // math.isqrt(rank ** skew) + 1 for rank in range(2, amount + 1)]
    surplus, given = total - most - (amount - 1), [1] * (amount - 1)
    while surplus > 0:
        movable = [i for i in range(amount - 1) if given[i] < most]
        whole, budget = sum([loads[i] for i in movable]), surplus
        for i in movable:
            extra = min(most - given[i], max(1, budget * loads[i] // whole), surplus)
            given[i] = given[i] + extra
            surplus = surplus - extra
    return np.array([most] + given)


def uneven_parts(own_key, amount, total, most, slope):
    if amount == 2:
        one = jax.random.randint(own_key, (), max(1, total - most), min(most, total - 1) + 1)
        return jnp.stack([one, total - one])
    sizes = jnp.asarray(split_up(amount, total, most, slope), jnp.int32)
    twos = (amount - 1) // 2
    giver, receiver = sizes[1:1 + 2 * twos:2], sizes[2:2 + 2 * twos:2]
    slack = jnp.minimum(giver - 1, most - receiver)
    passed = jax.random.randint(jax.random.fold_in(own_key, 1), (twos,), 0, 1 << 20) % (slack + 1)
    sizes = sizes.at[1:1 + 2 * twos:2].set(giver - passed).at[2:2 + 2 * twos:2].set(receiver + passed)
    return sizes[jax.random.permutation(jax.random.fold_in(own_key, 2), amount)]


def setup_inputs(seed: int = 0) -> dict:
    seeds = jax.random.split(jax.random.key(seed), 9)
    images = draw_images(jax.random.fold_in(seeds[8], 71), 0)
    projections = draw_projections(jax.random.fold_in(seeds[8], 71), 0)
    ctf_table = draw_ctf_table(jax.random.fold_in(seeds[8], 71), 0)
    ctf_group = draw_ctf_group(jax.random.fold_in(seeds[8], 71), 0)
    orient_ids = draw_orient_ids(jax.random.fold_in(seeds[8], 71), 0)
    trans_ids = draw_trans_ids(jax.random.fold_in(seeds[8], 71), 0)
    inv_sigma = jnp.clip(jnp.exp(math.log(2.0) - 1.3862944 * jax.random.uniform(seeds[6], (2, FC), jnp.float32) ** block_scale(seeds[6], (2, FC), ((0, 2),), -0.2, 0.2)), 0.5, 2.0)
    counts = jax.vmap(lambda own: uneven_parts(own, SHARDS, LIVE, PART_DEV, 1))(jax.random.split(seeds[7], 2)).reshape((2, SHARDS)).astype(jnp.int32)
    return {"images": images, "projections": projections, "ctf_table": ctf_table, "ctf_group": ctf_group, "orient_ids": orient_ids, "trans_ids": trans_ids, "inv_sigma": inv_sigma, "counts": counts}


def phases(trans_list, start, count):
    half_width = BOX // 2 + 1
    freq_index = start + jnp.arange(count, dtype=jnp.int32)
    row_index = freq_index // half_width
    col_index = freq_index % half_width
    wave_x = (row_index - BOX * (row_index >= BOX // 2).astype(jnp.int32)).astype(jnp.float32)
    wave_y = col_index.astype(jnp.float32)
    shift_x = (trans_list % TGRID - TGRID // 2).astype(jnp.float32)
    shift_y = (trans_list // TGRID - TGRID // 2).astype(jnp.float32)
    angle = (2.0 * math.pi / BOX) * (shift_x[:, None] * wave_x[None, :] + shift_y[:, None] * wave_y[None, :])
    return jnp.cos(angle), jnp.sin(angle)


def shift_sections(sections, inverse, cosine, sine):
    real_part = sections[:, :, 0, :].astype(jnp.float32) * inverse
    imag_part = sections[:, :, 1, :].astype(jnp.float32) * inverse
    shifted_re = real_part[:, :, None, :] * cosine - imag_part[:, :, None, :] * sine
    shifted_im = real_part[:, :, None, :] * sine + imag_part[:, :, None, :] * cosine
    return jnp.stack([shifted_re, shifted_im], axis=3).astype(jnp.bfloat16)


def section_power(sections):
    real_part = sections[:, :, 0, :].astype(jnp.float32)
    imag_part = sections[:, :, 1, :].astype(jnp.float32)
    total = real_part * real_part + imag_part * imag_part
    return total.reshape(-1, total.shape[-1])


def contract_last(left, right):
    return lax.dot_general(left, right, (((1,), (1,)), ((), ())), preferred_element_type=jnp.float32)


def contract_high(left, right):
    return lax.dot_general(left, right, (((1,), (1,)), ((), ())), precision=lax.Precision.HIGHEST, preferred_element_type=jnp.float32)


def reference(images, projections, ctf_table, ctf_group, orient_ids, trans_ids, inv_sigma, counts):
    posts = []
    slabs = []
    for half_index in range(2):
        groups_here = ctf_group[half_index]
        ctf_rows = ctf_table[half_index][groups_here]
        weighted = (ctf_rows[:, None, :] * images[half_index].astype(jnp.float32)).astype(jnp.bfloat16)
        flat_images = weighted.reshape(PARTICLES, 2 * FC)
        cosine, sine = phases(trans_ids[half_index], 0, FC)
        inverse = inv_sigma[half_index]
        ctf_power = ctf_table[half_index] * ctf_table[half_index] * inverse

        def score_class(class_sections):
            shifted = shift_sections(class_sections[None], inverse, cosine, sine).reshape(O * TR, 2 * FC)
            cross_terms = contract_last(flat_images, shifted)
            norm_table = contract_high(ctf_power, section_power(class_sections[None]))
            return cross_terms.reshape(PARTICLES, O, TR) - 0.5 * norm_table[groups_here][:, :, None]

        scores = jnp.moveaxis(lax.map(score_class, projections[half_index]), 0, 1)
        allowed = jnp.any(orient_ids[half_index][:, :, None] == jnp.arange(O, dtype=jnp.int32)[None, None, :], axis=1)
        mask = jnp.broadcast_to(allowed[:, None, :, None], scores.shape)
        top = jnp.max(jnp.where(mask, scores, -jnp.inf), axis=(1, 2, 3), keepdims=True)
        expo = jnp.exp(jnp.where(mask, scores - top, -jnp.inf))
        total = jnp.sum(expo, axis=(1, 2, 3), keepdims=True)
        slot_index = jnp.arange(PARTICLES, dtype=jnp.int32)
        live = (slot_index % PART_DEV < counts[half_index][slot_index // PART_DEV]).astype(jnp.float32)
        weights = (expo / total * live[:, None, None, None]).astype(jnp.bfloat16)
        posts.append(weights.reshape(PARTICLES, K * O * TR))
        per_class = jnp.moveaxis(weights, 1, 0).reshape(K, PARTICLES, O * TR)

        def back_class(class_weights):
            summed = lax.dot_general(class_weights, flat_images, (((0,), (0,)), ((), ())), preferred_element_type=jnp.float32)
            summed = summed.reshape(O, TR, 2, FC)
            slab_re = jnp.sum(summed[:, :, 0] * cosine + summed[:, :, 1] * sine, axis=1)
            slab_im = jnp.sum(summed[:, :, 1] * cosine - summed[:, :, 0] * sine, axis=1)
            return jnp.stack([slab_re, slab_im], axis=1)

        slabs.append(lax.map(back_class, per_class))
    product = slabs[0][:, :, 0] * slabs[1][:, :, 0] + slabs[0][:, :, 1] * slabs[1][:, :, 1]
    return jnp.stack(posts), jnp.stack(slabs), jnp.stack([product, product])
```

```python
import functools
import math

import jax
import jax.numpy as jnp
from jax import lax
from jax.experimental import pallas as pl
from jax.experimental.pallas import tpu as pltpu
from jax.sharding import PartitionSpec as P

BOX = 128
O = 8
TGRID = 5


def phases(trans_list, count):
    half_width = BOX // 2 + 1
    freq_index = jnp.arange(count, dtype=jnp.int32)
    row_index = freq_index // half_width
    col_index = freq_index % half_width
    wave_x = (row_index - BOX * (row_index >= BOX // 2).astype(jnp.int32)).astype(jnp.float32)
    wave_y = col_index.astype(jnp.float32)
    shift_x = (trans_list % TGRID - TGRID // 2).astype(jnp.float32)
    shift_y = (trans_list // TGRID - TGRID // 2).astype(jnp.float32)
    angle = (
        2.0
        * math.pi
        / BOX
        * (shift_x[:, None] * wave_x[None, :] + shift_y[:, None] * wave_y[None, :])
    )
    return (jnp.cos(angle), jnp.sin(angle))


def flip_img(value):
    return lax.ppermute(value, "img", [(i, i ^ 1) for i in range(lax.axis_size("img"))])


def flip_cls(value):
    return lax.ppermute(value, "cls", [(i, i ^ 1) for i in range(lax.axis_size("cls"))])


def rotate_img(value, step):
    lines = lax.axis_size("img") // 2
    perm = [(i, (i // 2 + step) % lines * 2 + i % 2) for i in range(2 * lines)]
    return lax.ppermute(value, "img", perm)


def add_rounded(left, right):
    return (left.astype(jnp.float32) + right.astype(jnp.float32)).astype(jnp.bfloat16)


def expectation_kernel(
    tile,
    place_ref,
    live_ref,
    group_ref,
    orient_ref,
    wre_ref,
    wim_ref,
    near_re,
    far_re,
    near_im,
    far_im,
    table_ref,
    inverse_ref,
    cos_ref,
    sin_ref,
    post_ref,
    out_near_re,
    out_far_re,
    out_near_im,
    out_far_im,
    sec_re,
    sec_im,
    shifted,
    cross,
    norm,
    slab_re,
    slab_im,
):
    rows, freqs = wre_ref.shape
    groups = table_ref.shape[0]
    trans = cos_ref.shape[0]
    _, lines, owned, width = near_re.shape
    sections = sec_re.shape[0]
    columns = sections * trans
    my_cls, my_line, my_side = place_ref[0], place_ref[1], place_ref[2]

    def place(j):
        step = lax.rem(my_line - j // 2 + lines, lines)
        side = lax.rem(my_side + j % 2, 2)
        return side, step

    for c in range(sections // owned):
        mine = my_cls == c
        for j in range(2 * lines):
            side, step = place(j)
            to = (slice(c * owned, (c + 1) * owned), slice(j * width, (j + 1) * width))
            sec_re[to] = jnp.where(mine, near_re[side, step], far_re[side, step])
            sec_im[to] = jnp.where(mine, near_im[side, step], far_im[side, step])

    cross[...] = jnp.zeros_like(cross)
    norm[...] = jnp.zeros_like(norm)

    @pl.loop(0, freqs // tile)
    def _(i):
        at = pl.ds(pl.multiple_of(i * tile, tile), tile)
        inverse = inverse_ref[:, at]
        real = sec_re[:, at].astype(jnp.float32)
        imag = sec_im[:, at].astype(jnp.float32)
        table = table_ref[:, at]
        norm[...] += lax.dot_general(
            table * table * inverse,
            real * real + imag * imag,
            (((1,), (1,)), ((), ())),
            precision=lax.Precision.HIGHEST,
            preferred_element_type=jnp.float32,
        )
        real = real * inverse
        imag = imag * inverse
        for t in range(trans):
            cosine = cos_ref[t : t + 1, at]
            sine = sin_ref[t : t + 1, at]
            to = slice(t * sections, (t + 1) * sections)
            shifted[to, :tile] = (real * cosine - imag * sine).astype(jnp.bfloat16)
            shifted[to, tile:] = (real * sine + imag * cosine).astype(jnp.bfloat16)
        images = jnp.concatenate([wre_ref[:, at], wim_ref[:, at]], axis=1)
        cross[...] += lax.dot_general(
            images,
            shifted[...],
            (((1,), (1,)), ((), ())),
            preferred_element_type=jnp.float32,
        )

    onehot = (
        group_ref[...] == lax.broadcasted_iota(jnp.int32, (rows, groups), 1)
    ).astype(jnp.float32)
    norm_rows = jnp.dot(
        onehot,
        jnp.concatenate([norm[...]] * trans, axis=1),
        precision=lax.Precision.HIGHEST,
        preferred_element_type=jnp.float32,
    )
    scores = cross[...] - 0.5 * norm_rows
    orient = lax.broadcasted_iota(jnp.int32, (rows, columns), 1) & (O - 1)
    ids = orient_ref[...]
    mask = ids[:, 0:1] == orient
    for n in range(1, ids.shape[1]):
        mask = mask | (ids[:, n : n + 1] == orient)
    top = jnp.max(jnp.where(mask, scores, -jnp.inf), axis=1, keepdims=True)
    expo = jnp.exp(jnp.where(mask, scores - top, -jnp.inf))
    total = jnp.sum(expo, axis=1, keepdims=True)
    live = (lax.broadcasted_iota(jnp.int32, (rows, 1), 0) < live_ref[0]).astype(jnp.float32)
    weights = expo / total * live
    rounded = weights.astype(jnp.bfloat16)
    source = lax.broadcasted_iota(jnp.int32, (columns, columns), 0)
    target = lax.broadcasted_iota(jnp.int32, (columns, columns), 1)
    reorder = (source == (target & (trans - 1)) * sections + target // trans).astype(
        jnp.float32
    ).astype(jnp.bfloat16)
    post_ref[...] = jnp.dot(rounded, reorder, preferred_element_type=jnp.float32).astype(
        jnp.bfloat16
    )
    turned = weights.T.astype(jnp.bfloat16)

    @pl.loop(0, freqs // tile)
    def _(i):
        at = pl.ds(pl.multiple_of(i * tile, tile), tile)
        image_re = wre_ref[:, at]
        image_im = wim_ref[:, at]
        total_re = jnp.zeros((sections, tile), jnp.float32)
        total_im = jnp.zeros((sections, tile), jnp.float32)
        for t in range(trans):
            cosine = cos_ref[t : t + 1, at]
            sine = sin_ref[t : t + 1, at]
            part = turned[t * sections : (t + 1) * sections]
            back_re = jnp.dot(part, image_re, preferred_element_type=jnp.float32)
            back_im = jnp.dot(part, image_im, preferred_element_type=jnp.float32)
            total_re += back_re * cosine + back_im * sine
            total_im += back_im * cosine - back_re * sine
        slab_re[:, at] = total_re.astype(jnp.bfloat16)
        slab_im[:, at] = total_im.astype(jnp.bfloat16)

    for c in range(sections // owned):
        mine = my_cls == c
        for j in range(2 * lines):
            side, step = place(j)
            at = (slice(c * owned, (c + 1) * owned), slice(j * width, (j + 1) * width))
            chunk_re = slab_re[at]
            chunk_im = slab_im[at]

            @pl.when(mine)
            def _():
                out_near_re[side, step] = chunk_re
                out_near_im[side, step] = chunk_im

            @pl.when(jnp.logical_not(mine))
            def _():
                out_far_re[side, step] = chunk_re
                out_far_im[side, step] = chunk_im


def on_device(images, projections, ctf_table, ctf_group, orient_ids, trans_ids, inv_sigma, counts):
    num_rows = images.shape[1]
    freqs = images.shape[3]
    groups = ctf_table.shape[1]
    _, classes, orients, _, width = projections.shape
    owned = classes * orients
    sections = owned * lax.axis_size("cls")
    lines = lax.axis_size("img") // 2
    trans = trans_ids.shape[1]
    columns = sections * trans
    tile = max(d for d in range(128, 641, 128) if freqs % d == 0)
    cls_index = lax.axis_index("cls")
    img_index = lax.axis_index("img")

    own = projections[0].reshape(owned, 2, width).transpose(1, 0, 2)
    line = jnp.stack([own] + [rotate_img(own, s) for s in range(1, lines)], axis=1)
    near_re = jnp.stack([line[0], flip_img(line[0])])
    near_im = jnp.stack([line[1], flip_cls(line[1])])
    far_re = flip_cls(near_re)
    other_im = flip_img(near_im)
    side_near_im = jnp.stack([near_im[0], other_im[0]])
    side_far_im = jnp.stack([near_im[1], other_im[1]])

    table = ctf_table[0]
    onehot = (ctf_group[0][:, None] == jnp.arange(groups, dtype=jnp.int32)[None, :]).astype(
        jnp.float32
    )
    ctf_rows = jnp.dot(
        onehot, table, precision=lax.Precision.HIGHEST, preferred_element_type=jnp.float32
    )
    weighted_re = (ctf_rows * images[0, :, 0].astype(jnp.float32)).astype(jnp.bfloat16)
    weighted_im = (ctf_rows * images[0, :, 1].astype(jnp.float32)).astype(jnp.bfloat16)
    cosine, sine = phases(trans_ids[0], freqs)

    place = jnp.stack([cls_index, img_index // 2, img_index % 2]).astype(jnp.int32)
    chunks = jax.ShapeDtypeStruct((2, lines, owned, width), jnp.bfloat16)
    vmem = pl.BlockSpec(memory_space=pltpu.VMEM)
    smem = pl.BlockSpec(memory_space=pltpu.SMEM)
    post, out_near_re, out_far_re, out_near_im, out_far_im = pl.pallas_call(
        functools.partial(expectation_kernel, tile),
        out_shape=[
            jax.ShapeDtypeStruct((num_rows, columns), jnp.bfloat16),
            chunks,
            chunks,
            chunks,
            chunks,
        ],
        in_specs=[smem, smem] + [vmem] * 12,
        out_specs=[vmem] * 5,
        scratch_shapes=[
            pltpu.VMEM((sections, freqs), jnp.bfloat16),
            pltpu.VMEM((sections, freqs), jnp.bfloat16),
            pltpu.VMEM((columns, 2 * tile), jnp.bfloat16),
            pltpu.VMEM((num_rows, columns), jnp.float32),
            pltpu.VMEM((groups, sections), jnp.float32),
            pltpu.VMEM((sections, freqs), jnp.bfloat16),
            pltpu.VMEM((sections, freqs), jnp.bfloat16),
        ],
        compiler_params=pltpu.CompilerParams(vmem_limit_bytes=50 * 1024 * 1024),
        cost_estimate=pl.CostEstimate(
            flops=8 * num_rows * columns * freqs,
            bytes_accessed=8 * num_rows * freqs,
            transcendentals=num_rows * columns,
        ),
    )(
        place,
        counts[0],
        ctf_group[0][:, None],
        orient_ids[0],
        weighted_re,
        weighted_im,
        near_re,
        far_re,
        side_near_im,
        side_far_im,
        table,
        inv_sigma,
        cosine,
        sine,
    )

    sum_re = add_rounded(out_near_re, flip_cls(out_far_re))
    away = flip_img(jnp.stack([out_near_im[1], out_far_im[1]]))
    sum_im = add_rounded(jnp.stack([out_near_im[0], out_far_im[0]]), away)
    line_re = add_rounded(sum_re[0], flip_img(sum_re[1]))
    line_im = add_rounded(sum_im[0], flip_cls(sum_im[1]))
    lines_both = jnp.stack([line_re, line_im], axis=1)
    own_slab = lines_both[0].astype(jnp.float32)
    for s in range(1, lines):
        own_slab = own_slab + rotate_img(lines_both[s], lines - s).astype(jnp.float32)
    partner = lax.ppermute(own_slab.astype(jnp.bfloat16), "half", [(0, 1), (1, 0)]).astype(
        jnp.float32
    )
    product = own_slab[0] * partner[0] + own_slab[1] * partner[1]
    slab = own_slab.transpose(1, 0, 2).reshape(classes, orients, 2, width)
    return (post[None], slab[None], product.reshape(classes, orients, width)[None])


def solution(mesh):
    return jax.shard_map(
        on_device,
        mesh=mesh,
        in_specs=(
            P("half", ("cls", "img"), None, None),
            P("half", "cls", None, None, "img"),
            P("half", None, None),
            P("half", ("cls", "img")),
            P("half", ("cls", "img"), None),
            P("half", None),
            P("half", None),
            P("half", ("cls", "img")),
        ),
        out_specs=(
            P("half", ("cls", "img"), None),
            P("half", "cls", None, None, "img"),
            P("half", "cls", None, "img"),
        ),
        check_vma=False,
    )
```

```python
import functools
import math

import jax
import jax.numpy as jnp
from jax import lax
from jax.experimental import pallas as pl
from jax.experimental.pallas import tpu as pltpu
from jax.sharding import PartitionSpec as P

BOX = 128
O = 8
TGRID = 5


def phases(trans_list, count):
    half_width = BOX // 2 + 1
    freq_index = jnp.arange(count, dtype=jnp.int32)
    row_index = freq_index // half_width
    col_index = freq_index % half_width
    wave_x = (row_index - BOX * (row_index >= BOX // 2).astype(jnp.int32)).astype(jnp.float32)
    wave_y = col_index.astype(jnp.float32)
    shift_x = (trans_list % TGRID - TGRID // 2).astype(jnp.float32)
    shift_y = (trans_list // TGRID - TGRID // 2).astype(jnp.float32)
    angle = (
        2.0
        * math.pi
        / BOX
        * (shift_x[:, None] * wave_x[None, :] + shift_y[:, None] * wave_y[None, :])
    )
    return (jnp.cos(angle), jnp.sin(angle))


def flip_img(value):
    return lax.ppermute(value, "img", [(i, i ^ 1) for i in range(lax.axis_size("img"))])


def flip_cls(value):
    return lax.ppermute(value, "cls", [(i, i ^ 1) for i in range(lax.axis_size("cls"))])


def rotate_img(value, step):
    lines = lax.axis_size("img") // 2
    perm = [(i, (i // 2 + step) % lines * 2 + i % 2) for i in range(2 * lines)]
    return lax.ppermute(value, "img", perm)


def add_rounded(left, right):
    return (left.astype(jnp.float32) + right.astype(jnp.float32)).astype(jnp.bfloat16)


def place(j, my_line, my_side, lines):
    return lax.rem(my_side + j % 2, 2), lax.rem(my_line - j // 2 + lines, lines)


def expectation_kernel(
    tile,
    place_ref,
    live_ref,
    group_ref,
    orient_ref,
    wre_ref,
    wim_ref,
    *refs,
):
    blocks_re, blocks_im = refs[:4], refs[4:8]
    table_ref, inverse_ref, cos_ref, sin_ref, post_ref, turned_ref = refs[8:14]
    sec_re, sec_im, shifted, cross, norm = refs[14:]
    freqs = wre_ref.shape[1]
    rows = group_ref.shape[0]
    groups = table_ref.shape[0]
    trans = cos_ref.shape[0]
    lines, owned, width = blocks_re[0].shape
    sections = sec_re.shape[0]
    columns = sections * trans
    my_cls, my_line, my_side = place_ref[0], place_ref[1], place_ref[2]

    for c in range(sections // owned):
        mine = my_cls == c
        for j in range(2 * lines):
            side, step = place(j, my_line, my_side, lines)
            to = (slice(c * owned, (c + 1) * owned), slice(j * width, (j + 1) * width))
            for section, blocks in ((sec_re, blocks_re), (sec_im, blocks_im)):
                near = jnp.where(side == 0, blocks[0][step], blocks[1][step])
                far = jnp.where(side == 0, blocks[2][step], blocks[3][step])
                section[to] = jnp.where(mine, near, far)

    cross[...] = jnp.zeros_like(cross)
    norm[...] = jnp.zeros_like(norm)

    @pl.loop(0, freqs // tile)
    def _(i):
        at = pl.ds(pl.multiple_of(i * tile, tile), tile)
        inverse = inverse_ref[:, at]
        real = sec_re[:, at].astype(jnp.float32)
        imag = sec_im[:, at].astype(jnp.float32)
        table = table_ref[:, at]
        norm[...] += lax.dot_general(
            table * table * inverse,
            real * real + imag * imag,
            (((1,), (1,)), ((), ())),
            precision=lax.Precision.HIGHEST,
            preferred_element_type=jnp.float32,
        )
        real = real * inverse
        imag = imag * inverse
        for t in range(trans):
            cosine = cos_ref[t : t + 1, at]
            sine = sin_ref[t : t + 1, at]
            to = slice(t * sections, (t + 1) * sections)
            shifted[to, :tile] = (real * cosine - imag * sine).astype(jnp.bfloat16)
            shifted[to, tile:] = (real * sine + imag * cosine).astype(jnp.bfloat16)
        images = jnp.concatenate([wre_ref[:, at], wim_ref[:, at]], axis=1)
        cross[...] += lax.dot_general(
            images,
            shifted[...],
            (((1,), (1,)), ((), ())),
            preferred_element_type=jnp.float32,
        )

    onehot = (
        group_ref[...] == lax.broadcasted_iota(jnp.int32, (rows, groups), 1)
    ).astype(jnp.float32)
    norm_rows = jnp.dot(
        onehot,
        jnp.concatenate([norm[...]] * trans, axis=1),
        precision=lax.Precision.HIGHEST,
        preferred_element_type=jnp.float32,
    )
    scores = cross[...] - 0.5 * norm_rows
    orient = lax.broadcasted_iota(jnp.int32, (rows, columns), 1) & (O - 1)
    ids = orient_ref[...]
    mask = ids[:, 0:1] == orient
    for n in range(1, ids.shape[1]):
        mask = mask | (ids[:, n : n + 1] == orient)
    top = jnp.max(jnp.where(mask, scores, -jnp.inf), axis=1, keepdims=True)
    expo = jnp.exp(jnp.where(mask, scores - top, -jnp.inf))
    total = jnp.sum(expo, axis=1, keepdims=True)
    live = (lax.broadcasted_iota(jnp.int32, (rows, 1), 0) < live_ref[0]).astype(jnp.float32)
    weights = expo / total * live
    rounded = weights.astype(jnp.bfloat16)
    source = lax.broadcasted_iota(jnp.int32, (columns, columns), 0)
    target = lax.broadcasted_iota(jnp.int32, (columns, columns), 1)
    reorder = (source == (target & (trans - 1)) * sections + target // trans).astype(
        jnp.float32
    ).astype(jnp.bfloat16)
    post_ref[...] = jnp.dot(rounded, reorder, preferred_element_type=jnp.float32).astype(
        jnp.bfloat16
    )
    turned_ref[...] = weights.T.astype(jnp.bfloat16)


def projection_kernel(
    tile,
    place_ref,
    turned_ref,
    wre_ref,
    wim_ref,
    cos_ref,
    sin_ref,
    out_re_same,
    out_re_other,
    out_im_same,
    out_im_other,
    slab_re,
    slab_im,
):
    freqs = wre_ref.shape[1]
    trans = cos_ref.shape[0]
    lines, owned, width = out_re_same.shape
    sections = turned_ref.shape[0] // trans
    my_line, my_side, chosen = place_ref[1], place_ref[2], place_ref[3]
    weights = jnp.concatenate(
        [
            turned_ref[pl.ds(pl.multiple_of(t * sections + chosen * owned, owned), owned)]
            for t in range(trans)
        ],
        axis=0,
    )

    @pl.loop(0, freqs // tile)
    def _(i):
        at = pl.ds(pl.multiple_of(i * tile, tile), tile)
        image_re = wre_ref[:, at]
        image_im = wim_ref[:, at]
        back_re = jnp.dot(weights, image_re, preferred_element_type=jnp.float32)
        back_im = jnp.dot(weights, image_im, preferred_element_type=jnp.float32)
        total_re = jnp.zeros((owned, tile), jnp.float32)
        total_im = jnp.zeros((owned, tile), jnp.float32)
        for t in range(trans):
            cosine = cos_ref[t : t + 1, at]
            sine = sin_ref[t : t + 1, at]
            part_re = back_re[t * owned : (t + 1) * owned]
            part_im = back_im[t * owned : (t + 1) * owned]
            total_re += part_re * cosine + part_im * sine
            total_im += part_im * cosine - part_re * sine
        slab_re[:, at] = total_re.astype(jnp.bfloat16)
        slab_im[:, at] = total_im.astype(jnp.bfloat16)

    for j in range(2 * lines):
        side, step = place(j, my_line, my_side, lines)
        chunk_re = slab_re[:, j * width : (j + 1) * width]
        chunk_im = slab_im[:, j * width : (j + 1) * width]

        @pl.when(side == 0)
        def _():
            out_re_same[step] = chunk_re
            out_im_same[step] = chunk_im

        @pl.when(side != 0)
        def _():
            out_re_other[step] = chunk_re
            out_im_other[step] = chunk_im


def on_device(images, projections, ctf_table, ctf_group, orient_ids, trans_ids, inv_sigma, counts):
    num_rows = images.shape[1]
    freqs = images.shape[3]
    groups = ctf_table.shape[1]
    _, classes, orients, _, width = projections.shape
    owned = classes * orients
    sections = owned * lax.axis_size("cls")
    lines = lax.axis_size("img") // 2
    trans = trans_ids.shape[1]
    columns = sections * trans
    tile = max(d for d in range(128, 641, 128) if freqs % d == 0)
    cls_index = lax.axis_index("cls")
    img_index = lax.axis_index("img")

    own = projections[0].reshape(owned, 2, width).transpose(1, 0, 2)
    line = jnp.stack([own] + [rotate_img(own, s) for s in range(1, lines)], axis=1)
    same_re, same_im = line[0], line[1]
    side_re = flip_img(same_re)
    far_im = flip_cls(same_im)
    far_re = flip_cls(same_re)
    side_im = flip_img(same_im)
    table, side_re, far_im = lax.optimization_barrier((ctf_table[0], side_re, far_im))
    blocks = [same_re, side_re, far_re, flip_cls(side_re)]
    blocks += [same_im, side_im, far_im, flip_img(far_im)]
    onehot = (ctf_group[0][:, None] == jnp.arange(groups, dtype=jnp.int32)[None, :]).astype(
        jnp.float32
    )
    ctf_rows = jnp.dot(
        onehot, table, precision=lax.Precision.HIGHEST, preferred_element_type=jnp.float32
    )
    weighted = [
        (ctf_rows * images[0, :, part].astype(jnp.float32)).astype(jnp.bfloat16)
        for part in range(2)
    ]
    cosine, sine = phases(trans_ids[0], freqs)

    place_mine = [cls_index, img_index // 2, img_index % 2]
    vmem = pl.BlockSpec(memory_space=pltpu.VMEM)
    smem = pl.BlockSpec(memory_space=pltpu.SMEM)
    post, turned = pl.pallas_call(
        functools.partial(expectation_kernel, tile),
        out_shape=[
            jax.ShapeDtypeStruct((num_rows, columns), jnp.bfloat16),
            jax.ShapeDtypeStruct((columns, num_rows), jnp.bfloat16),
        ],
        in_specs=[smem, smem] + [vmem] * 16,
        out_specs=[vmem] * 2,
        scratch_shapes=[
            pltpu.VMEM((sections, freqs), jnp.bfloat16),
            pltpu.VMEM((sections, freqs), jnp.bfloat16),
            pltpu.VMEM((columns, 2 * tile), jnp.bfloat16),
            pltpu.VMEM((num_rows, columns), jnp.float32),
            pltpu.VMEM((groups, sections), jnp.float32),
        ],
        compiler_params=pltpu.CompilerParams(vmem_limit_bytes=40 * 1024 * 1024),
        cost_estimate=pl.CostEstimate(
            flops=4 * num_rows * columns * freqs,
            bytes_accessed=4 * num_rows * freqs,
            transcendentals=num_rows * columns,
        ),
    )(
        jnp.stack(place_mine).astype(jnp.int32),
        counts[0],
        ctf_group[0][:, None],
        orient_ids[0],
        *weighted,
        *blocks,
        table,
        inv_sigma,
        cosine,
        sine,
    )

    def project(chosen):
        chunks = jax.ShapeDtypeStruct((lines, owned, width), jnp.bfloat16)
        return pl.pallas_call(
            functools.partial(projection_kernel, tile),
            out_shape=[chunks] * 4,
            in_specs=[smem] + [vmem] * 5,
            out_specs=[vmem] * 4,
            scratch_shapes=[
                pltpu.VMEM((owned, freqs), jnp.bfloat16),
                pltpu.VMEM((owned, freqs), jnp.bfloat16),
            ],
            compiler_params=pltpu.CompilerParams(vmem_limit_bytes=40 * 1024 * 1024),
            cost_estimate=pl.CostEstimate(
                flops=num_rows * columns * freqs // 8,
                bytes_accessed=4 * num_rows * freqs,
                transcendentals=0,
            ),
        )(jnp.stack(place_mine + [chosen]).astype(jnp.int32), turned, *weighted, cosine, sine)

    far_re_same, far_re_other, far_im_same, far_im_other = project(1 - cls_index)
    near_re_same, near_re_other, near_im_same, near_im_other = project(cls_index)

    other_re = add_rounded(near_re_other, flip_cls(far_re_other))
    sum_im_far = add_rounded(far_im_same, flip_img(far_im_other))
    same_sum = add_rounded(near_re_same, flip_cls(far_re_same))
    sum_im_near = add_rounded(near_im_same, flip_img(near_im_other))
    line_re = add_rounded(same_sum, flip_img(other_re))
    line_im = add_rounded(sum_im_near, flip_cls(sum_im_far))
    lines_both = jnp.stack([line_re, line_im], axis=1)
    own_slab = lines_both[0].astype(jnp.float32)
    for s in range(1, lines):
        own_slab = own_slab + rotate_img(lines_both[s], lines - s).astype(jnp.float32)
    partner = lax.ppermute(own_slab.astype(jnp.bfloat16), "half", [(0, 1), (1, 0)]).astype(
        jnp.float32
    )
    product = own_slab[0] * partner[0] + own_slab[1] * partner[1]
    slab = own_slab.transpose(1, 0, 2).reshape(classes, orients, 2, width)
    return (post[None], slab[None], product.reshape(classes, orients, width)[None])


def solution(mesh):
    return jax.shard_map(
        on_device,
        mesh=mesh,
        in_specs=(
            P("half", ("cls", "img"), None, None),
            P("half", "cls", None, None, "img"),
            P("half", None, None),
            P("half", ("cls", "img")),
            P("half", ("cls", "img"), None),
            P("half", None),
            P("half", None),
            P("half", ("cls", "img")),
        ),
        out_specs=(
            P("half", ("cls", "img"), None),
            P("half", "cls", None, None, "img"),
            P("half", "cls", None, "img"),
        ),
        check_vma=False,
    )
```

```python
import functools
import math

import jax
import jax.numpy as jnp
from jax import lax
from jax.experimental import pallas as pl
from jax.experimental.pallas import tpu as pltpu
from jax.sharding import PartitionSpec as P

BOX = 128
O = 8
TGRID = 5


def phases(trans_list, count):
    half_width = BOX // 2 + 1
    freq_index = jnp.arange(count, dtype=jnp.int32)
    row_index = freq_index // half_width
    col_index = freq_index % half_width
    wave_x = (row_index - BOX * (row_index >= BOX // 2).astype(jnp.int32)).astype(jnp.float32)
    wave_y = col_index.astype(jnp.float32)
    shift_x = (trans_list % TGRID - TGRID // 2).astype(jnp.float32)
    shift_y = (trans_list // TGRID - TGRID // 2).astype(jnp.float32)
    angle = (
        2.0
        * math.pi
        / BOX
        * (shift_x[:, None] * wave_x[None, :] + shift_y[:, None] * wave_y[None, :])
    )
    return (jnp.cos(angle), jnp.sin(angle))


def flip_img(value):
    return lax.ppermute(value, "img", [(i, i ^ 1) for i in range(lax.axis_size("img"))])


def flip_cls(value):
    return lax.ppermute(value, "cls", [(i, i ^ 1) for i in range(lax.axis_size("cls"))])


def rotate_img(value, step):
    lines = lax.axis_size("img") // 2
    perm = [(i, (i // 2 + step) % lines * 2 + i % 2) for i in range(2 * lines)]
    return lax.ppermute(value, "img", perm)


def add_rounded(left, right):
    return (left.astype(jnp.float32) + right.astype(jnp.float32)).astype(jnp.bfloat16)


def place(j, my_line, my_side, lines):
    return lax.rem(my_side + j % 2, 2), lax.rem(my_line - j // 2 + lines, lines)


def expectation_kernel(
    tile,
    place_ref,
    live_ref,
    group_ref,
    orient_ref,
    wre_ref,
    wim_ref,
    *refs,
):
    blocks_re, blocks_im = refs[:4], refs[4:8]
    table_ref, inverse_ref, cos_ref, sin_ref, post_ref, turned_ref = refs[8:14]
    sec_re, sec_im, shifted, cross, norm = refs[14:]
    freqs = wre_ref.shape[1]
    rows = group_ref.shape[0]
    groups = table_ref.shape[0]
    trans = cos_ref.shape[0]
    lines, owned, width = blocks_re[0].shape
    sections = sec_re.shape[0]
    columns = sections * trans
    my_cls, my_line, my_side = place_ref[0], place_ref[1], place_ref[2]

    for c in range(sections // owned):
        mine = my_cls == c
        for j in range(2 * lines):
            side, step = place(j, my_line, my_side, lines)
            to = (slice(c * owned, (c + 1) * owned), slice(j * width, (j + 1) * width))
            for section, blocks in ((sec_re, blocks_re), (sec_im, blocks_im)):
                near = jnp.where(side == 0, blocks[0][step], blocks[1][step])
                far = jnp.where(side == 0, blocks[2][step], blocks[3][step])
                section[to] = jnp.where(mine, near, far)

    cross[...] = jnp.zeros_like(cross)
    norm[...] = jnp.zeros_like(norm)

    @pl.loop(0, freqs // tile)
    def _(i):
        at = pl.ds(pl.multiple_of(i * tile, tile), tile)
        inverse = inverse_ref[:, at]
        real = sec_re[:, at].astype(jnp.float32)
        imag = sec_im[:, at].astype(jnp.float32)
        table = table_ref[:, at]
        norm[...] += lax.dot_general(
            table * table * inverse,
            real * real + imag * imag,
            (((1,), (1,)), ((), ())),
            precision=lax.Precision.HIGHEST,
            preferred_element_type=jnp.float32,
        )
        real = real * inverse
        imag = imag * inverse
        for t in range(trans):
            cosine = cos_ref[t : t + 1, at]
            sine = sin_ref[t : t + 1, at]
            to = slice(t * sections, (t + 1) * sections)
            shifted[to, :tile] = (real * cosine - imag * sine).astype(jnp.bfloat16)
            shifted[to, tile:] = (real * sine + imag * cosine).astype(jnp.bfloat16)
        images = jnp.concatenate([wre_ref[:, at], wim_ref[:, at]], axis=1)
        cross[...] += lax.dot_general(
            images,
            shifted[...],
            (((1,), (1,)), ((), ())),
            preferred_element_type=jnp.float32,
        )

    onehot = (
        group_ref[...] == lax.broadcasted_iota(jnp.int32, (rows, groups), 1)
    ).astype(jnp.float32)
    norm_rows = jnp.dot(
        onehot,
        jnp.concatenate([norm[...]] * trans, axis=1),
        precision=lax.Precision.HIGHEST,
        preferred_element_type=jnp.float32,
    )
    scores = cross[...] - 0.5 * norm_rows
    orient = lax.broadcasted_iota(jnp.int32, (rows, columns), 1) & (O - 1)
    ids = orient_ref[...]
    mask = ids[:, 0:1] == orient
    for n in range(1, ids.shape[1]):
        mask = mask | (ids[:, n : n + 1] == orient)
    top = jnp.max(jnp.where(mask, scores, -jnp.inf), axis=1, keepdims=True)
    expo = jnp.exp(jnp.where(mask, scores - top, -jnp.inf))
    total = jnp.sum(expo, axis=1, keepdims=True)
    live = (lax.broadcasted_iota(jnp.int32, (rows, 1), 0) < live_ref[0]).astype(jnp.float32)
    weights = expo / total * live
    rounded = weights.astype(jnp.bfloat16)
    source = lax.broadcasted_iota(jnp.int32, (columns, columns), 0)
    target = lax.broadcasted_iota(jnp.int32, (columns, columns), 1)
    reorder = (source == (target & (trans - 1)) * sections + target // trans).astype(
        jnp.float32
    ).astype(jnp.bfloat16)
    post_ref[...] = jnp.dot(rounded, reorder, preferred_element_type=jnp.float32).astype(
        jnp.bfloat16
    )
    turned_ref[...] = weights.T.astype(jnp.bfloat16)


def projection_kernel(
    tile,
    place_ref,
    turned_ref,
    wre_ref,
    wim_ref,
    cos_ref,
    sin_ref,
    out_same,
    out_other,
    slab_re,
    slab_im,
):
    freqs = wre_ref.shape[1]
    trans = cos_ref.shape[0]
    lines, _, owned, width = out_same.shape
    sections = turned_ref.shape[0] // trans
    my_line, my_side, chosen = place_ref[1], place_ref[2], place_ref[3]
    weights = jnp.concatenate(
        [
            turned_ref[pl.ds(pl.multiple_of(t * sections + chosen * owned, owned), owned)]
            for t in range(trans)
        ],
        axis=0,
    )

    @pl.loop(0, freqs // tile)
    def _(i):
        at = pl.ds(pl.multiple_of(i * tile, tile), tile)
        image_re = wre_ref[:, at]
        image_im = wim_ref[:, at]
        back_re = jnp.dot(weights, image_re, preferred_element_type=jnp.float32)
        back_im = jnp.dot(weights, image_im, preferred_element_type=jnp.float32)
        total_re = jnp.zeros((owned, tile), jnp.float32)
        total_im = jnp.zeros((owned, tile), jnp.float32)
        for t in range(trans):
            cosine = cos_ref[t : t + 1, at]
            sine = sin_ref[t : t + 1, at]
            part_re = back_re[t * owned : (t + 1) * owned]
            part_im = back_im[t * owned : (t + 1) * owned]
            total_re += part_re * cosine + part_im * sine
            total_im += part_im * cosine - part_re * sine
        slab_re[:, at] = total_re.astype(jnp.bfloat16)
        slab_im[:, at] = total_im.astype(jnp.bfloat16)

    for j in range(2 * lines):
        side, step = place(j, my_line, my_side, lines)
        chunk_re = slab_re[:, j * width : (j + 1) * width]
        chunk_im = slab_im[:, j * width : (j + 1) * width]

        @pl.when(side == 0)
        def _():
            out_same[step, 0] = chunk_re
            out_same[step, 1] = chunk_im

        @pl.when(side != 0)
        def _():
            out_other[step, 0] = chunk_re
            out_other[step, 1] = chunk_im


def on_device(images, projections, ctf_table, ctf_group, orient_ids, trans_ids, inv_sigma, counts):
    num_rows = images.shape[1]
    freqs = images.shape[3]
    groups = ctf_table.shape[1]
    _, classes, orients, _, width = projections.shape
    owned = classes * orients
    sections = owned * lax.axis_size("cls")
    lines = lax.axis_size("img") // 2
    trans = trans_ids.shape[1]
    columns = sections * trans
    tile = max(d for d in range(128, 641, 128) if freqs % d == 0)
    cls_index = lax.axis_index("cls")
    img_index = lax.axis_index("img")

    own = projections[0].reshape(owned, 2, width).transpose(1, 0, 2)
    line = jnp.stack([own] + [rotate_img(own, s) for s in range(1, lines)], axis=1)
    early_table, line = lax.optimization_barrier((ctf_table[0], line))
    same_re, same_im = line[0], line[1]
    side_re = flip_img(same_re)
    far_im = flip_cls(same_im)
    far_re = flip_cls(same_re)
    side_im = flip_img(same_im)
    table, side_re, far_im = lax.optimization_barrier((ctf_table[0], side_re, far_im))
    blocks = [same_re, side_re, far_re, flip_cls(side_re)]
    blocks += [same_im, side_im, far_im, flip_img(far_im)]
    onehot = (ctf_group[0][:, None] == jnp.arange(groups, dtype=jnp.int32)[None, :]).astype(
        jnp.float32
    )
    weighted = []
    for part, values in enumerate((table, early_table)):
        ctf_rows = jnp.dot(
            onehot, values, precision=lax.Precision.HIGHEST, preferred_element_type=jnp.float32
        )
        weighted.append(
            (ctf_rows * images[0, :, part].astype(jnp.float32)).astype(jnp.bfloat16)
        )
    cosine, sine = phases(trans_ids[0], freqs)

    place_mine = [cls_index, img_index // 2, img_index % 2]
    vmem = pl.BlockSpec(memory_space=pltpu.VMEM)
    smem = pl.BlockSpec(memory_space=pltpu.SMEM)
    post, turned = pl.pallas_call(
        functools.partial(expectation_kernel, tile),
        out_shape=[
            jax.ShapeDtypeStruct((num_rows, columns), jnp.bfloat16),
            jax.ShapeDtypeStruct((columns, num_rows), jnp.bfloat16),
        ],
        in_specs=[smem, smem] + [vmem] * 16,
        out_specs=[vmem] * 2,
        scratch_shapes=[
            pltpu.VMEM((sections, freqs), jnp.bfloat16),
            pltpu.VMEM((sections, freqs), jnp.bfloat16),
            pltpu.VMEM((columns, 2 * tile), jnp.bfloat16),
            pltpu.VMEM((num_rows, columns), jnp.float32),
            pltpu.VMEM((groups, sections), jnp.float32),
        ],
        compiler_params=pltpu.CompilerParams(vmem_limit_bytes=40 * 1024 * 1024),
        cost_estimate=pl.CostEstimate(
            flops=4 * num_rows * columns * freqs,
            bytes_accessed=4 * num_rows * freqs,
            transcendentals=num_rows * columns,
        ),
    )(
        jnp.stack(place_mine).astype(jnp.int32),
        counts[0],
        ctf_group[0][:, None],
        orient_ids[0],
        *weighted,
        *blocks,
        table,
        inv_sigma,
        cosine,
        sine,
    )

    def project(chosen):
        chunks = jax.ShapeDtypeStruct((lines, 2, owned, width), jnp.bfloat16)
        return pl.pallas_call(
            functools.partial(projection_kernel, tile),
            out_shape=[chunks] * 2,
            in_specs=[smem] + [vmem] * 5,
            out_specs=[vmem] * 2,
            scratch_shapes=[
                pltpu.VMEM((owned, freqs), jnp.bfloat16),
                pltpu.VMEM((owned, freqs), jnp.bfloat16),
            ],
            compiler_params=pltpu.CompilerParams(vmem_limit_bytes=40 * 1024 * 1024),
            cost_estimate=pl.CostEstimate(
                flops=num_rows * columns * freqs // 8,
                bytes_accessed=4 * num_rows * freqs,
                transcendentals=0,
            ),
        )(jnp.stack(place_mine + [chosen]).astype(jnp.int32), turned, *weighted, cosine, sine)

    far_same, far_other = project(1 - cls_index)
    near_same, near_other = project(cls_index)
    sum_far = add_rounded(far_same, flip_img(far_other))
    sum_near = add_rounded(near_same, flip_img(near_other))
    lines_both = add_rounded(sum_near, flip_cls(sum_far))
    own_slab = lines_both[0].astype(jnp.float32)
    for s in range(1, lines):
        own_slab = own_slab + rotate_img(lines_both[s], lines - s).astype(jnp.float32)
    partner = lax.ppermute(own_slab.astype(jnp.bfloat16), "half", [(0, 1), (1, 0)]).astype(
        jnp.float32
    )
    product = own_slab[0] * partner[0] + own_slab[1] * partner[1]
    slab = own_slab.transpose(1, 0, 2).reshape(classes, orients, 2, width)
    return (post[None], slab[None], product.reshape(classes, orients, width)[None])


def solution(mesh):
    return jax.shard_map(
        on_device,
        mesh=mesh,
        in_specs=(
            P("half", ("cls", "img"), None, None),
            P("half", "cls", None, None, "img"),
            P("half", None, None),
            P("half", ("cls", "img")),
            P("half", ("cls", "img"), None),
            P("half", None),
            P("half", None),
            P("half", ("cls", "img")),
        ),
        out_specs=(
            P("half", ("cls", "img"), None),
            P("half", "cls", None, None, "img"),
            P("half", "cls", None, "img"),
        ),
        check_vma=False,
    )
```
